512 devices in a mesh: dp: 32 (over z, x), tensor: 16 (over y, core).
Axes of the slice: x: 4, y: 8, z: 8, core: 2. Of those that a mesh axis runs over, the one named last changes fastest.
Arguments:
- tokens: bfloat16 [512, 8192], P('dp', 'tensor'), may hold values from -6 to 6
- cotangent: bfloat16 [512, 8192], P('dp', 'tensor'), may hold values from -6 to 6
- token_class: int32 [512], P('dp'), may hold values from 0 to 3
- class_bands: int32 [4], replicated, may hold values from 1 to 32, as said below
- mantissas: bfloat16 [3, 28672, 8192], P(None, 'dp', 'tensor'), may hold values from -0.0625 to 0.0625
- exponents: int32 [3, 224, 64], P(None, 'dp', 'tensor'), may hold values from -2 to 1
Outputs:
- mixed: bfloat16 [512, 8192], P('dp', 'tensor')
- input_grad: bfloat16 [512, 8192], P('dp', 'tensor')
- down_grad: bfloat16 [28672, 8192], P('dp', 'tensor')
The draws below stay inside these ranges and needn't reach their ends.
Inputs may be any that keep to these rules, and one draw needn't show every extreme that they name: `class_bands`: some class uses all 32 bands.
All inputs are finite; a program needn't handle non-finite values.
Results may differ from the reference program's by a relative error of at most 0.0085.
Values may be sent and summed in bfloat16 or wider, within the bound.
No kernel may reach another device: no remote copies, remote signals or barrier semaphores. Data moves between devices by JAX's collectives and lax.ppermute only.
A program may use at most 64 MiB of HBM per device.

```python
import jax
import jax.numpy as jnp

D = 8192
FF_BAND = 896
BLOCK = 128
NCLASS = 4
BANDS = 32
FF = 28672
TOKENS = 512


def draw_class_bands(key, part):
    key = jax.random.fold_in(key, 5)
    first_key, second_key = jax.random.split(key)
    values = jax.random.randint(first_key, (NCLASS,), 1, BANDS + 1)
    spot = jax.random.randint(second_key, (), 0, NCLASS)
    values = jnp.where(jnp.arange(NCLASS) == spot, BANDS, values)
    return values.astype(jnp.int32)


def with_ends(drawn, rng, smallest, largest):
    longest = drawn.shape.index(max(drawn.shape))
    spots = []
    for shift in (0, 1):
        where = [jax.random.randint(jax.random.fold_in(rng, axis), (), 0, length) for axis, length in enumerate(drawn.shape)]
        where[longest] = (where[longest] + shift) % drawn.shape[longest]
        spots.append(tuple(where))
    return drawn.at[spots[0]].set(smallest).at[spots[1]].set(largest)


def block_scale(key, dims, cuts, smallest, high):
    def one(position, blocks):
        steps = jax.random.uniform(jax.random.fold_in(jax.random.fold_in(key, 6), position), (blocks,), jnp.float32, smallest / len(cuts), high / len(cuts))
        return jnp.repeat(jnp.exp(steps), dims[position] // blocks).reshape((-1,) + (1,) * (len(dims) - position - 1))

    level = one(*cuts[0])
    for cut in cuts[1:]:
        level = level * one(*cut)
    return level


def noise(rng, extent, deviation, limit, cuts=(), kind=jnp.bfloat16):
    level = block_scale(rng, extent, cuts, -0.22, 0.18) if cuts else 1.0
    entries = jax.random.normal(rng, extent, jnp.float32) * deviation * level
    return jnp.minimum(jnp.maximum(entries, -limit), limit).astype(kind)


def setup_inputs(seed: int = 0) -> dict:
    keys = jax.random.split(jax.random.key(seed), 7)
    tokens = noise(keys[0], (TOKENS, D), 1.0, 6.0, ((0, 32), (1, 16)))
    cotangent = noise(keys[1], (TOKENS, D), 1.0, 6.0, ((0, 32), (1, 16)))
    token_class = with_ends(jax.random.randint(keys[2], (TOKENS,), 0, NCLASS), jax.random.fold_in(keys[2], 1), 0, NCLASS - 1).astype(jnp.int32)
    class_bands = draw_class_bands(jax.random.fold_in(keys[6], 71), 0)
    mantissas = noise(keys[4], (3, FF, D), D ** -0.5, 0.0625, ((1, 32), (2, 16)))
    exponents = with_ends(jax.random.randint(keys[5], (3, FF // BLOCK, D // BLOCK), -2, 2), jax.random.fold_in(keys[5], 1), -2, 1).astype(jnp.int32)
    return dict(tokens=tokens, cotangent=cotangent, token_class=token_class, class_bands=class_bands, mantissas=mantissas, exponents=exponents)


def dequant(mant, expo):
    rows, cols = mant.shape
    scale = jnp.exp2(expo.astype(jnp.float32)).astype(mant.dtype)
    blocks = mant.reshape(rows // BLOCK, BLOCK, cols // BLOCK, BLOCK) * scale[:, None, :, None]
    return blocks.reshape(rows, cols)

def reference(tokens, cotangent, token_class, class_bands, mantissas, exponents):
    gate_w = dequant(mantissas[0], exponents[0])
    up_w = dequant(mantissas[1], exponents[1])
    down_w = dequant(mantissas[2], exponents[2])
    width = class_bands[token_class] * FF_BAND
    units = jnp.arange(FF, dtype=jnp.int32)
    keep = (units[None, :] < width[:, None]).astype(jnp.float32)
    gate = jnp.dot(tokens, gate_w.T, preferred_element_type=jnp.float32)
    up = jnp.dot(tokens, up_w.T, preferred_element_type=jnp.float32)
    sig = jax.nn.sigmoid(gate)
    silu = gate * sig
    hidden = (keep * silu * up).astype(jnp.bfloat16)
    mixed = jnp.dot(hidden, down_w, preferred_element_type=jnp.float32).astype(jnp.bfloat16)
    dh = jnp.dot(cotangent, down_w.T, preferred_element_type=jnp.float32)
    dgate = (keep * dh * up * sig * (1.0 + gate * (1.0 - sig))).astype(jnp.bfloat16)
    dup = (keep * dh * silu).astype(jnp.bfloat16)
    input_grad = (jnp.dot(dgate, gate_w, preferred_element_type=jnp.float32) + jnp.dot(dup, up_w, preferred_element_type=jnp.float32)).astype(jnp.bfloat16)
    norm_factor = 1.0 / jnp.sqrt(jnp.float32(TOKENS))
    down_grad = (jnp.dot(hidden.T, cotangent, preferred_element_type=jnp.float32) * norm_factor).astype(jnp.bfloat16)
    return (mixed, input_grad, down_grad)
```

```python
import jax
import jax.numpy as jnp
from jax import lax
from jax.experimental import pallas as pl
from jax.experimental.pallas import tpu as pltpu
from jax.sharding import Mesh
from jax.sharding import PartitionSpec as P

BLOCK = 128
SWAP = [(0, 1), (1, 0)]
NT = (((1,), (1,)), ((), ()))
TN = (((0,), (0,)), ((), ()))
F32 = jnp.float32
BF16 = jnp.bfloat16


def call(kernel, name, outs, args, smem=(), flops=0, moved=0):
    vmem = pl.BlockSpec(memory_space=pltpu.VMEM)
    scalar = pl.BlockSpec(memory_space=pltpu.SMEM)
    return pl.pallas_call(
        kernel,
        name=name,
        out_shape=outs,
        in_specs=[scalar if i in smem else vmem for i in range(len(args))],
        out_specs=vmem,
        cost_estimate=pl.CostEstimate(flops=flops, bytes_accessed=moved, transcendentals=0),
        compiler_params=pltpu.CompilerParams(vmem_limit_bytes=32 * 1024 * 1024),
    )(*args)


def dequant_kernel(scale, mant, out):
    mats, rows, cols = mant.shape
    for m in range(mats):
        for r in range(rows // BLOCK):
            for c in range(cols // BLOCK):
                at = (m, pl.ds(r * BLOCK, BLOCK), pl.ds(c * BLOCK, BLOCK))
                out[at] = (mant[at].astype(F32) * scale[m, r, c]).astype(BF16)


def project_kernel(tokens, own, other, out):
    senders, rows, width = tokens.shape
    half = width // 2
    units = own.shape[1]
    wide = tokens[...].astype(F32).reshape(senders, 2, rows // 2, width)
    x = wide[:, 0].reshape(-1, width).astype(BF16)
    dy = wide[:, 1].reshape(-1, width).astype(BF16)
    for m, left in ((0, x), (1, x), (2, dy)):
        term = lax.dot_general(left[:, :half], own[m], NT, preferred_element_type=F32)
        term += lax.dot_general(left[:, half:], other[m], NT, preferred_element_type=F32)
        out[:, :, m * units : (m + 1) * units] = term.astype(BF16).reshape(out.shape[0], out.shape[1], units)


def activate_kernel(parts, out):
    copies, _, three = parts.shape
    units = three // 3
    total = jnp.sum(parts[...].astype(F32), axis=0)
    gate, up, dh = total[:, :units], total[:, units : 2 * units], total[:, 2 * units :]
    sig = jax.nn.sigmoid(gate)
    silu = gate * sig
    hidden = (silu * up).astype(BF16)
    dgate = (dh * up * sig * (1.0 + gate * (1.0 - sig))).astype(BF16)
    dup = (dh * silu).astype(BF16)
    for i in range(copies):
        out[i, :, :units] = hidden
        out[i, :, units : 2 * units] = dgate
        out[i, :, 2 * units :] = dup


def expand_kernel(acts, own, other, out):
    units = own.shape[1]
    owners, rows, width = out.shape
    half = width // 2
    hidden = acts[:, :, :units].reshape(-1, units)
    dgate = acts[:, :, units : 2 * units].reshape(-1, units)
    dup = acts[:, :, 2 * units :].reshape(-1, units)
    for start, w in ((0, own), (half, other)):
        mixed = jnp.dot(hidden, w[2], preferred_element_type=F32)
        grad = jnp.dot(dgate, w[0], preferred_element_type=F32)
        grad += jnp.dot(dup, w[1], preferred_element_type=F32)
        both = jnp.concatenate(
            [mixed.reshape(owners, rows // 2, half), grad.reshape(owners, rows // 2, half)], axis=1
        )
        out[:, :, start : start + half] = both.astype(BF16)


def body(tokens, cotangent, token_class, class_bands, mantissas, exponents):
    bands = lax.axis_size("dp")
    lines = lax.axis_size("y")
    core = lax.axis_index("c")
    rows, half = tokens.shape
    mine = rows // 2
    units = mantissas.shape[1]

    pair = jnp.stack([tokens.reshape(2, mine, half), cotangent.reshape(2, mine, half)], axis=1)
    keep_part = lax.dynamic_index_in_dim(pair, core, 0, False).reshape(rows, half)
    send_part = lax.dynamic_index_in_dim(pair, 1 - core, 0, False).reshape(rows, half)
    got_part = lax.ppermute(send_part, "c", SWAP)
    block = jnp.concatenate([keep_part, got_part], axis=1)
    classes = lax.dynamic_slice_in_dim(token_class, core * mine, mine)
    lookup = classes[:, None] == jnp.arange(class_bands.shape[0], dtype=jnp.int32)[None, :]
    used = jnp.sum(jnp.where(lookup, class_bands[None, :], 0), axis=1)
    used = jnp.concatenate([used, used])
    band = jnp.arange(bands, dtype=jnp.int32)
    masked = jnp.where((band[:, None] < used[None, :])[:, :, None], block[None], 0)
    gathered = lax.all_to_all(masked, "dp", 0, 0, tiled=True)

    scale = jnp.exp2(exponents.astype(F32)).astype(BF16).astype(F32)
    own = call(dequant_kernel, "dequant", jax.ShapeDtypeStruct(mantissas.shape, BF16), (scale, mantissas),
               smem=(0,), flops=mantissas.size, moved=4 * mantissas.size)
    other = lax.ppermute(own, "c", SWAP)

    count = bands * mine
    work = 2 * count * 3 * units * 2 * half
    parts = call(project_kernel, "project", jax.ShapeDtypeStruct((lines, count // lines, 3 * units), BF16),
                 (gathered, own, other), flops=work, moved=10 << 20)
    parts = lax.all_to_all(parts, "y", 0, 0, tiled=True)
    acts = call(activate_kernel, "activate", jax.ShapeDtypeStruct(parts.shape, BF16), (parts,),
                flops=parts.size, moved=4 * parts.size)
    acts = lax.all_to_all(acts, "y", 0, 0, tiled=True)
    terms = call(expand_kernel, "expand", jax.ShapeDtypeStruct((bands, rows, 2 * half), BF16),
                 (acts, own, other), flops=work, moved=10 << 20)
    terms = lax.all_to_all(terms, "dp", 0, 0, tiled=True)

    hidden = acts[:, :, :units].reshape(count, units)
    dy = gathered[:, mine:, :].reshape(count, 2 * half)
    norm_factor = 1.0 / jnp.sqrt(jnp.float32(2 * count))
    down = lax.dot_general(hidden, dy[:, :half], TN, preferred_element_type=F32)
    away = lax.dot_general(hidden, dy[:, half:], TN, preferred_element_type=F32).astype(BF16)
    away = lax.ppermute(away, "c", SWAP)
    down_grad = ((down + away.astype(F32)) * norm_factor).astype(BF16)

    total = jnp.sum(terms.astype(F32), axis=0).astype(BF16)
    kept = total[:, :half].reshape(2, mine, half)
    got = lax.ppermute(total[:, half:], "c", SWAP).reshape(2, mine, half)
    first = jnp.where(core == 0, kept, got)
    last = jnp.where(core == 0, got, kept)
    both = jnp.concatenate([first, last], axis=1)
    return both[0], both[1], down_grad


def solution(mesh):
    dp, tensor = mesh.devices.shape
    split = Mesh(mesh.devices.reshape(dp, tensor // 2, 2), ("dp", "y", "c"))
    cols = ("y", "c")
    in_specs = (
        P("dp", cols),
        P("dp", cols),
        P("dp"),
        P(),
        P(None, "dp", cols),
        P(None, "dp", cols),
    )
    out_specs = (P("dp", cols), P("dp", cols), P("dp", cols))
    return jax.shard_map(body, mesh=split, in_specs=in_specs, out_specs=out_specs, check_vma=False)
```

```python
import jax
import jax.numpy as jnp
from jax import lax
from jax.experimental import pallas as pl
from jax.experimental.pallas import tpu as pltpu
from jax.sharding import Mesh
from jax.sharding import PartitionSpec as P

BLOCK = 128
X_CHIPS = 4
SWAP = [(0, 1), (1, 0)]
NT = (((1,), (1,)), ((), ()))
TN = (((0,), (0,)), ((), ()))
F32 = jnp.float32
BF16 = jnp.bfloat16


def call(kernel, name, outs, args, smem=(), flops=0, moved=0):
    vmem = pl.BlockSpec(memory_space=pltpu.VMEM)
    scalar = pl.BlockSpec(memory_space=pltpu.SMEM)
    return pl.pallas_call(
        kernel,
        name=name,
        out_shape=outs,
        in_specs=[scalar if i in smem else vmem for i in range(len(args))],
        out_specs=jax.tree.map(lambda _: vmem, outs),
        cost_estimate=pl.CostEstimate(flops=flops, bytes_accessed=moved, transcendentals=0),
        compiler_params=pltpu.CompilerParams(vmem_limit_bytes=32 * 1024 * 1024),
    )(*args)


def dequant_kernel(scale, mant, out):
    mats, rows, cols = mant.shape
    for m in range(mats):
        for r in range(rows // BLOCK):
            for c in range(cols // BLOCK):
                at = (m, pl.ds(r * BLOCK, BLOCK), pl.ds(c * BLOCK, BLOCK))
                out[at] = (mant[at].astype(F32) * scale[m, r, c]).astype(BF16)


def gather_kernel(used, tokens, cotangent, out):
    rows, half = tokens.shape
    mine = rows // 2
    x, dy = tokens[...].astype(F32), cotangent[...].astype(F32)
    for c in range(2):
        at = slice(c * mine, (c + 1) * mine)
        block = jnp.concatenate([x[at], dy[at]], axis=0).astype(BF16)
        counts = used[at].astype(F32)
        tail = jnp.broadcast_to(jnp.concatenate([counts, counts], axis=0), (rows, BLOCK)).astype(BF16)
        for i in range(c, out.shape[0], 2):
            out[i, :, :half] = block
            out[i, :, half:] = tail


def spread_kernel(place, near, out):
    copies, chips, _, width = out.shape
    half = width // 2
    for i in range(chips):
        own = near[2 * i + place[0], :, :half].astype(F32)
        other = near[2 * i + 1 - place[0], :, :half].astype(F32)
        limit = near[2 * i, :, half:].astype(F32)[:, :1]
        for x in range(copies):
            keep = (place[1] * copies + x).astype(F32) < limit
            out[x, i, :, :half] = jnp.where(keep, own, 0.0).astype(BF16)
            out[x, i, :, half:] = jnp.where(keep, other, 0.0).astype(BF16)


def project_kernel(part, tokens, own, other, dy_out, keep, top, low):
    senders, rows, width = tokens.shape
    some = senders // 2
    half = width // 2
    units = own.shape[1]
    groups, chunk = keep.shape[:2]

    def split(h):
        wide = tokens[pl.ds(h * some, some)].astype(F32).reshape(some, 2, rows // 2, width)
        return [wide[:, i].reshape(-1, width) for i in range(2)]

    near, far = split(part[0]), split(1 - part[0])
    x, dy = [jnp.concatenate([far[i], near[i]], axis=0).astype(BF16) for i in range(2)]
    dy_out[...] = dy
    for m, left in ((0, x), (1, x), (2, dy)):
        term = lax.dot_general(left[:, :half], own[m], NT, preferred_element_type=F32)
        term += lax.dot_general(left[:, half:], other[m], NT, preferred_element_type=F32)
        term = term.astype(BF16).reshape(2 * groups, chunk, units)
        at = slice(m * units, (m + 1) * units)
        top[:, :, at] = term[:groups, : chunk // 2]
        low[:, :, at] = term[:groups, chunk // 2 :]
        keep[:, :, at] = term[groups:]


def activate_kernel(parts, out):
    copies, _, three = parts.shape
    units = three // 3
    total = jnp.sum(parts[...].astype(F32), axis=0)
    gate, up, dh = total[:, :units], total[:, units : 2 * units], total[:, 2 * units :]
    sig = jax.nn.sigmoid(gate)
    silu = gate * sig
    hidden = (silu * up).astype(BF16)
    dgate = (dh * up * sig * (1.0 + gate * (1.0 - sig))).astype(BF16)
    dup = (dh * silu).astype(BF16)
    for i in range(copies):
        out[i, :, :units] = hidden
        out[i, :, units : 2 * units] = dgate
        out[i, :, 2 * units :] = dup


def expand_kernel(part, acts, top, low, own, other, out, hidden_out):
    units = own.shape[1]
    owners, rows, width = out.shape
    some = owners // 2
    half = width // 2
    tokens = hidden_out.shape[0] // 2
    far = jnp.concatenate([top[...], low[...]], axis=1)
    for i, (h, left) in enumerate(((1 - part[0], far), (part[0], acts[...]))):
        left = left.reshape(tokens, 3 * units)
        hidden, dgate, dup = left[:, :units], left[:, units : 2 * units], left[:, 2 * units :]
        hidden_out[i * tokens : (i + 1) * tokens] = hidden
        for start, w in ((0, own), (half, other)):
            mixed = jnp.dot(hidden, w[2], preferred_element_type=F32)
            grad = jnp.dot(dgate, w[0], preferred_element_type=F32)
            grad += jnp.dot(dup, w[1], preferred_element_type=F32)
            both = jnp.concatenate(
                [mixed.reshape(some, rows // 2, half), grad.reshape(some, rows // 2, half)], axis=1
            )
            out[pl.ds(h * some, some), :, start : start + half] = both.astype(BF16)


def by_core(core, a, b):
    return jnp.where(core == 0, a, b), jnp.where(core == 0, b, a)


def body(tokens, cotangent, token_class, class_bands, mantissas, exponents):
    zs, xs, ks = lax.axis_size("z"), lax.axis_size("x"), lax.axis_size("k")
    lines = 2 * ks
    core = lax.axis_index("c")
    odd = lax.axis_index("p").reshape(1)
    rows, half = tokens.shape
    mine = rows // 2
    mats, units = mantissas.shape[:2]
    bands = zs * xs
    count = bands * mine
    chunk = count // lines
    left_pairs = [(i, i ^ 1) for i in range(lines)]
    right_pairs = [(i, (i + 1 if i % 2 else i - 1) % lines) for i in range(lines)]

    def swap_near(top, low):
        return (lax.ppermute(top, ("k", "p"), left_pairs), lax.ppermute(low, ("k", "p"), right_pairs))

    lookup = token_class[:, None] == jnp.arange(class_bands.shape[0], dtype=jnp.int32)[None, :]
    used = jnp.sum(jnp.where(lookup, class_bands[None, :], 0), axis=1, keepdims=True)
    pair = call(gather_kernel, "gather", jax.ShapeDtypeStruct((zs * 2, rows, half + BLOCK), BF16),
                (used, tokens, cotangent), moved=1 << 18)
    pair, mantissas, exponents = lax.optimization_barrier((pair, mantissas, exponents))
    near = lax.all_to_all(pair, ("z", "c"), 0, 0, tiled=True)

    raw_other, exponents_other = lax.ppermute(mantissas, "c", SWAP), lax.ppermute(exponents, "c", SWAP)

    def dequant(raw, powers, name):
        scale = jnp.exp2(powers.astype(F32)).astype(BF16).astype(F32)
        return call(dequant_kernel, name, jax.ShapeDtypeStruct(raw.shape, BF16), (scale, raw),
                    smem=(0,), flops=raw.size, moved=4 * raw.size)

    own = dequant(mantissas, exponents, "dequant_own")
    other = dequant(raw_other, exponents_other, "dequant_other")

    place = jnp.stack([core, lax.axis_index("z")])
    near, own, other, odd, place = lax.optimization_barrier((near, own, other, odd, place))
    masked = call(spread_kernel, "spread", jax.ShapeDtypeStruct((xs, zs, rows, 2 * half), BF16), (place, near),
                  smem=(0,), moved=2 << 20)
    gathered = lax.all_to_all(masked, "x", 0, 0, tiled=True).reshape(bands, rows, 2 * half)

    work = count * mats * units * 2 * half

    def shape(*dims):
        return jax.ShapeDtypeStruct(dims, BF16)

    wide = mats * units
    dy, keep, *send = call(
        project_kernel, "project",
        (shape(count, 2 * half), shape(ks, chunk, wide)) + (shape(ks, chunk // 2, wide),) * 2,
        (odd, gathered, own, other), smem=(0,), flops=2 * work, moved=10 << 20)
    got = jnp.concatenate(swap_near(*send), axis=1)
    parts = (keep.astype(F32) + got.astype(F32)).astype(BF16)
    parts = lax.all_to_all(parts, "k", 0, 0, tiled=True)
    acts = call(activate_kernel, "activate", shape(*parts.shape), (parts,), flops=parts.size, moved=4 * parts.size)
    acts = lax.all_to_all(acts, "k", 0, 0, tiled=True)
    top, low = swap_near(acts[:, : chunk // 2], acts[:, chunk // 2 :])
    terms, hidden = call(expand_kernel, "expand", (shape(bands, rows, 2 * half), shape(count, units)),
                         (odd, acts, top, low, own, other), smem=(0,), flops=2 * work, moved=10 << 20)

    terms = lax.all_to_all(terms.reshape(xs, zs, rows, 2 * half), "x", 0, 0, tiled=True)
    terms = jnp.sum(terms.astype(F32), axis=0).astype(BF16)
    here, away = by_core(core, terms[:, :, :half], terms[:, :, half:])
    terms = jnp.stack([here, away], axis=1).reshape(zs * 2, rows, half)
    terms = lax.all_to_all(terms, ("z", "c"), 0, 0, tiled=True).reshape(zs, 2, rows, half)
    total = jnp.sum(terms.astype(F32), axis=0).astype(BF16)
    mixed = total[:, :mine].reshape(rows, half)
    input_grad = total[:, mine:].reshape(rows, half)

    norm_factor = 1.0 / jnp.sqrt(jnp.float32(2 * count))
    down = lax.dot_general(hidden, dy[:, :half], TN, preferred_element_type=F32)
    away = lax.dot_general(hidden, dy[:, half:], TN, preferred_element_type=F32).astype(BF16)
    away = lax.ppermute(away, "c", SWAP)
    down_grad = ((down + away.astype(F32)) * norm_factor).astype(BF16)
    return mixed, input_grad, down_grad


def solution(mesh):
    dp, tensor = mesh.devices.shape
    split = Mesh(mesh.devices.reshape(dp // X_CHIPS, X_CHIPS, tensor // 4, 2, 2), ("z", "x", "k", "p", "c"))
    toks, cols = ("z", "x"), ("k", "p", "c")
    in_specs = (
        P(toks, cols),
        P(toks, cols),
        P(toks),
        P(),
        P(None, toks, cols),
        P(None, toks, cols),
    )
    out_specs = (P(toks, cols), P(toks, cols), P(toks, cols))
    return jax.shard_map(body, mesh=split, in_specs=in_specs, out_specs=out_specs, check_vma=False)
```

```python
import jax
import jax.numpy as jnp
from jax import lax
from jax.experimental import pallas as pl
from jax.experimental.pallas import tpu as pltpu
from jax.sharding import Mesh
from jax.sharding import PartitionSpec as P

BLOCK = 128
X_CHIPS = 4
SWAP = [(0, 1), (1, 0)]
NT = (((1,), (1,)), ((), ()))
TN = (((0,), (0,)), ((), ()))
F32 = jnp.float32
BF16 = jnp.bfloat16


def call(kernel, name, outs, args, smem=(), flops=0, moved=0):
    vmem = pl.BlockSpec(memory_space=pltpu.VMEM)
    scalar = pl.BlockSpec(memory_space=pltpu.SMEM)
    return pl.pallas_call(
        kernel,
        name=name,
        out_shape=outs,
        in_specs=[scalar if i in smem else vmem for i in range(len(args))],
        out_specs=jax.tree.map(lambda _: vmem, outs),
        cost_estimate=pl.CostEstimate(flops=flops, bytes_accessed=moved, transcendentals=0),
        compiler_params=pltpu.CompilerParams(vmem_limit_bytes=32 * 1024 * 1024),
    )(*args)


def dequant_kernel(scale, mant, out):
    mats, rows, cols = mant.shape
    for m in range(mats):
        for r in range(rows // BLOCK):
            for c in range(cols // BLOCK):
                at = (m, pl.ds(r * BLOCK, BLOCK), pl.ds(c * BLOCK, BLOCK))
                out[at] = (mant[at].astype(F32) * scale[m, r, c]).astype(BF16)


def spread_kernel(place, near, out):
    copies, chips, _, width = out.shape
    half = width // 2
    for i in range(chips):
        own = near[2 * i + place[0], :, :half].astype(F32)
        other = near[2 * i + 1 - place[0], :, :half].astype(F32)
        limit = near[2 * i, :, half:].astype(F32)[:, :1]
        for x in range(copies):
            keep = (place[1] * copies + x).astype(F32) < limit
            out[x, i, :, :half] = jnp.where(keep, own, 0.0).astype(BF16)
            out[x, i, :, half:] = jnp.where(keep, other, 0.0).astype(BF16)


def project_kernel(part, tokens, own, other, dy_own, dy_other, keep, send):
    senders, rows, width = tokens.shape
    some = senders // 2
    half = width // 2
    units = own.shape[1]
    groups, chunk = keep.shape[0], keep.shape[1] // 3

    def split(h):
        wide = tokens[pl.ds(h * some, some)].astype(F32).reshape(some, 2, rows // 2, width)
        return [wide[:, i].reshape(-1, width) for i in range(2)]

    near, far = split(part[0]), split(1 - part[0])
    x, dy = [jnp.concatenate([far[i], near[i]], axis=0).astype(BF16) for i in range(2)]
    dy_own[...] = dy[:, :half]
    dy_other[...] = dy[:, half:]
    for m, left in ((0, x), (1, x), (2, dy)):
        term = lax.dot_general(left[:, :half], own[m], NT, preferred_element_type=F32)
        term += lax.dot_general(left[:, half:], other[m], NT, preferred_element_type=F32)
        term = term.astype(BF16).reshape(2 * groups, chunk, units)
        at = slice(m * chunk, (m + 1) * chunk)
        send[:, at] = term[:groups]
        keep[:, at] = term[groups:]


def activate_kernel(parts, out):
    copies, three, _ = parts.shape
    chunk = three // 3
    total = jnp.sum(parts[...].astype(F32), axis=0)
    gate, up, dh = total[:chunk], total[chunk : 2 * chunk], total[2 * chunk :]
    sig = jax.nn.sigmoid(gate)
    silu = gate * sig
    hidden = (silu * up).astype(BF16)
    dgate = (dh * up * sig * (1.0 + gate * (1.0 - sig))).astype(BF16)
    dup = (dh * silu).astype(BF16)
    for i in range(copies):
        out[i, :chunk] = hidden
        out[i, chunk : 2 * chunk] = dgate
        out[i, 2 * chunk :] = dup


def expand_kernel(part, acts, top, low, own, other, out, hidden_out):
    units = own.shape[1]
    owners, rows, width = out.shape
    some = owners // 2
    half = width // 2
    tokens = hidden_out.shape[0] // 2
    chunk = acts.shape[1] // 3
    groups = top.shape[0]
    for i, (h, parts) in enumerate(((1 - part[0], (top, low)), (part[0], (acts.at[:groups], acts.at[groups:])))):
        hidden, dgate, dup = [
            jnp.concatenate([p[:, j * chunk : (j + 1) * chunk].reshape(-1, units) for p in parts], axis=0) for j in range(3)
        ]
        hidden_out[i * tokens : (i + 1) * tokens] = hidden
        for start, w in ((0, own), (half, other)):
            mixed = jnp.dot(hidden, w[2], preferred_element_type=F32)
            grad = jnp.dot(dgate, w[0], preferred_element_type=F32)
            grad += jnp.dot(dup, w[1], preferred_element_type=F32)
            both = jnp.concatenate(
                [mixed.reshape(some, rows // 2, half), grad.reshape(some, rows // 2, half)], axis=1
            )
            out[pl.ds(h * some, some), :, start : start + half] = both.astype(BF16)


def gather_sum_kernel(core, terms, out):
    half = out.shape[2]
    total = jnp.sum(terms[...].astype(F32), axis=0).astype(BF16)
    for i in range(total.shape[0]):
        out[2 * i + core[0]] = total[i, :, :half]
        out[2 * i + 1 - core[0]] = total[i, :, half:]


def body(tokens, cotangent, token_class, class_bands, mantissas, exponents):
    zs, xs, ks = lax.axis_size("z"), lax.axis_size("x"), lax.axis_size("k")
    lines = 2 * ks
    core = lax.axis_index("c")
    odd = lax.axis_index("p").reshape(1)
    rows, half = tokens.shape
    mine = rows // 2
    mats, units = mantissas.shape[:2]
    bands = zs * xs
    count = bands * mine
    chunk = count // lines
    left_pairs = [(i, i ^ 1) for i in range(lines)]
    right_pairs = [(i, (i + 1 if i % 2 else i - 1) % lines) for i in range(lines)]

    pairs = [
        (2 * src + c, 2 * dst + c) for c, swaps in enumerate((left_pairs, right_pairs)) for src, dst in swaps
    ]

    def swap_near(top, low):
        return (lax.ppermute(top, ("k", "p"), left_pairs), lax.ppermute(low, ("k", "p"), right_pairs))

    lookup = token_class[:, None] == jnp.arange(class_bands.shape[0], dtype=jnp.int32)[None, :]
    used = jnp.sum(jnp.where(lookup, class_bands[None, :], 0), axis=1).astype(BF16).reshape(2, mine, 1)
    tail = jnp.broadcast_to(jnp.concatenate([used, used], axis=1), (2, rows, BLOCK))
    pair = jnp.concatenate([tokens.reshape(2, mine, half), cotangent.reshape(2, mine, half)], axis=1)
    pair = jnp.concatenate([pair, tail], axis=2)
    pair = jnp.broadcast_to(pair[None], (zs, 2, rows, half + BLOCK)).reshape(zs * 2, rows, half + BLOCK)
    pair, mantissas, exponents = lax.optimization_barrier((pair, mantissas, exponents))
    near = lax.all_to_all(pair, ("z", "c"), 0, 0, tiled=True)

    raw_other, exponents_other = lax.ppermute(mantissas, "c", SWAP), lax.ppermute(exponents, "c", SWAP)

    def dequant(raw, powers, name):
        scale = jnp.exp2(powers.astype(F32)).astype(BF16).astype(F32)
        return call(dequant_kernel, name, jax.ShapeDtypeStruct(raw.shape, BF16), (scale, raw),
                    smem=(0,), flops=raw.size, moved=4 * raw.size)

    own = dequant(mantissas, exponents, "dequant_own")
    other = dequant(raw_other, exponents_other, "dequant_other")

    place = jnp.stack([core, lax.axis_index("z")])
    near, own, other, odd, place = lax.optimization_barrier((near, own, other, odd, place))
    masked = call(spread_kernel, "spread", jax.ShapeDtypeStruct((xs, zs, rows, 2 * half), BF16), (place, near),
                  smem=(0,), moved=2 << 20)
    gathered = lax.all_to_all(masked, "x", 0, 0, tiled=True).reshape(bands, rows, 2 * half)

    work = count * mats * units * 2 * half

    def shape(*dims):
        return jax.ShapeDtypeStruct(dims, BF16)

    dy_own, dy_other, keep, send = call(
        project_kernel, "project", (shape(count, half),) * 2 + (shape(ks, 3 * chunk, units),) * 2,
        (odd, gathered, own, other), smem=(0,), flops=2 * work, moved=10 << 20)
    parts = (keep.astype(F32) + lax.ppermute(send, ("k", "p", "c"), pairs).astype(F32)).astype(BF16)
    parts = lax.all_to_all(parts, "k", 0, 0, tiled=True)
    acts = call(activate_kernel, "activate", shape(*parts.shape), (parts,), flops=parts.size, moved=4 * parts.size)
    acts = lax.all_to_all(acts, "k", 0, 0, tiled=True)
    top, low = swap_near(acts[: ks // 2], acts[ks // 2 :])
    terms, hidden = call(expand_kernel, "expand", (shape(bands, rows, 2 * half), shape(count, units)),
                         (odd, acts, top, low, own, other), smem=(0,), flops=2 * work, moved=10 << 20)

    terms = lax.all_to_all(terms.reshape(xs, zs, rows, 2 * half), "x", 0, 0, tiled=True)
    terms = call(gather_sum_kernel, "gather_sum", shape(zs * 2, rows, half), (core.reshape(1), terms),
                 smem=(0,), moved=1 << 20)
    terms, hidden, dy_other = lax.optimization_barrier((terms, hidden, dy_other))
    terms = lax.all_to_all(terms, ("z", "c"), 0, 0, tiled=True).reshape(zs, 2, rows, half)
    total = jnp.sum(terms.astype(F32), axis=0).astype(BF16)
    mixed = total[:, :mine].reshape(rows, half)
    input_grad = total[:, mine:].reshape(rows, half)

    norm_factor = 1.0 / jnp.sqrt(jnp.float32(2 * count))
    dy_got, got = lax.ppermute(dy_other, "c", SWAP), lax.ppermute(hidden, "c", SWAP)
    down = lax.dot_general(jnp.concatenate([hidden, got]), jnp.concatenate([dy_own, dy_got]), TN,
                           preferred_element_type=F32)
    down_grad = (down * norm_factor).astype(BF16)
    return mixed, input_grad, down_grad


def solution(mesh):
    dp, tensor = mesh.devices.shape
    split = Mesh(mesh.devices.reshape(dp // X_CHIPS, X_CHIPS, tensor // 4, 2, 2), ("z", "x", "k", "p", "c"))
    toks, cols = ("z", "x"), ("k", "p", "c")
    in_specs = (
        P(toks, cols),
        P(toks, cols),
        P(toks),
        P(),
        P(None, toks, cols),
        P(None, toks, cols),
    )
    out_specs = (P(toks, cols), P(toks, cols), P(toks, cols))
    return jax.shard_map(body, mesh=split, in_specs=in_specs, out_specs=out_specs, check_vma=False)
```

```python
import jax
import jax.numpy as jnp
from jax import lax
from jax.experimental import pallas as pl
from jax.experimental.pallas import tpu as pltpu
from jax.sharding import Mesh
from jax.sharding import PartitionSpec as P

BLOCK = 128
X_CHIPS = 4
SWAP = [(0, 1), (1, 0)]
NT = (((1,), (1,)), ((), ()))
TN = (((0,), (0,)), ((), ()))
F32 = jnp.float32
BF16 = jnp.bfloat16


def call(kernel, name, outs, args, smem=(), flops=0, moved=0):
    vmem = pl.BlockSpec(memory_space=pltpu.VMEM)
    scalar = pl.BlockSpec(memory_space=pltpu.SMEM)
    return pl.pallas_call(
        kernel,
        name=name,
        out_shape=outs,
        in_specs=[scalar if i in smem else vmem for i in range(len(args))],
        out_specs=jax.tree.map(lambda _: vmem, outs),
        cost_estimate=pl.CostEstimate(flops=flops, bytes_accessed=moved, transcendentals=0),
        compiler_params=pltpu.CompilerParams(vmem_limit_bytes=32 * 1024 * 1024),
    )(*args)


def dequant_kernel(scale, mant, out):
    mats, rows, cols = mant.shape
    for m in range(mats):
        for r in range(rows // BLOCK):
            for c in range(cols // BLOCK):
                at = (m, pl.ds(r * BLOCK, BLOCK), pl.ds(c * BLOCK, BLOCK))
                out[at] = (mant[at].astype(F32) * scale[m, r, c]).astype(BF16)


def spread_kernel(place, class_bands, near, out):
    copies, chips, _, width = out.shape
    half = width // 2
    for i in range(chips):
        own = near[2 * i + place[0], :, :half].astype(F32)
        other = near[2 * i + 1 - place[0], :, :half].astype(F32)
        kind = near[2 * i, :, half:].astype(F32)[:, :1]
        limit = jnp.zeros_like(kind)
        for j in range(class_bands.shape[0]):
            limit = jnp.where(kind == j, class_bands[j].astype(F32), limit)
        for x in range(copies):
            keep = (place[1] * copies + x).astype(F32) < limit
            out[x, i, :, :half] = jnp.where(keep, own, 0.0).astype(BF16)
            out[x, i, :, half:] = jnp.where(keep, other, 0.0).astype(BF16)


def project_kernel(part, tokens, own, other, dy_own, dy_other, keep, send):
    senders, rows, width = tokens.shape
    some = senders // 2
    half = width // 2
    units = own.shape[1]
    groups, chunk = keep.shape[0], keep.shape[1] // 3

    def split(h):
        wide = tokens[pl.ds(h * some, some)].astype(F32).reshape(some, 2, rows // 2, width)
        return [wide[:, i].reshape(-1, width) for i in range(2)]

    near, far = split(part[0]), split(1 - part[0])
    x, dy = [jnp.concatenate([far[i], near[i]], axis=0).astype(BF16) for i in range(2)]
    dy_own[...] = dy[:, :half]
    dy_other[...] = dy[:, half:]
    for m, left in ((0, x), (1, x), (2, dy)):
        term = lax.dot_general(left[:, :half], own[m], NT, preferred_element_type=F32)
        term += lax.dot_general(left[:, half:], other[m], NT, preferred_element_type=F32)
        term = term.astype(BF16).reshape(2 * groups, chunk, units)
        at = slice(m * chunk, (m + 1) * chunk)
        send[:, at] = term[:groups]
        keep[:, at] = term[groups:]


def activate_kernel(parts, out):
    copies, three, _ = parts.shape
    chunk = three // 3
    total = jnp.sum(parts[...].astype(F32), axis=0)
    gate, up, dh = total[:chunk], total[chunk : 2 * chunk], total[2 * chunk :]
    sig = jax.nn.sigmoid(gate)
    silu = gate * sig
    hidden = (silu * up).astype(BF16)
    dgate = (dh * up * sig * (1.0 + gate * (1.0 - sig))).astype(BF16)
    dup = (dh * silu).astype(BF16)
    for i in range(copies):
        out[i, :chunk] = hidden
        out[i, chunk : 2 * chunk] = dgate
        out[i, 2 * chunk :] = dup


def expand_kernel(part, acts, top, low, own, other, out, hidden_out):
    units = own.shape[1]
    owners, rows, width = out.shape
    some = owners // 2
    half = width // 2
    tokens = hidden_out.shape[0] // 2
    chunk = acts.shape[1] // 3
    groups = top.shape[0]
    for i, (h, parts) in enumerate(((1 - part[0], (top, low)), (part[0], (acts.at[:groups], acts.at[groups:])))):
        hidden, dgate, dup = [
            jnp.concatenate([p[:, j * chunk : (j + 1) * chunk].reshape(-1, units) for p in parts], axis=0) for j in range(3)
        ]
        hidden_out[i * tokens : (i + 1) * tokens] = hidden
        for start, w in ((0, own), (half, other)):
            mixed = jnp.dot(hidden, w[2], preferred_element_type=F32)
            grad = jnp.dot(dgate, w[0], preferred_element_type=F32)
            grad += jnp.dot(dup, w[1], preferred_element_type=F32)
            both = jnp.concatenate(
                [mixed.reshape(some, rows // 2, half), grad.reshape(some, rows // 2, half)], axis=1
            )
            out[pl.ds(h * some, some), :, start : start + half] = both.astype(BF16)


def gather_sum_kernel(core, terms, out):
    half = out.shape[2]
    total = jnp.sum(terms[...].astype(F32), axis=0).astype(BF16)
    for i in range(total.shape[0]):
        out[2 * i + core[0]] = total[i, :, :half]
        out[2 * i + 1 - core[0]] = total[i, :, half:]


def body(tokens, cotangent, token_class, class_bands, mantissas, exponents):
    zs, xs, ks = lax.axis_size("z"), lax.axis_size("x"), lax.axis_size("k")
    lines = 2 * ks
    core = lax.axis_index("c")
    odd = lax.axis_index("p").reshape(1)
    rows, half = tokens.shape
    mine = rows // 2
    mats, units = mantissas.shape[:2]
    bands = zs * xs
    count = bands * mine
    chunk = count // lines
    left_pairs = [(i, i ^ 1) for i in range(lines)]
    right_pairs = [(i, (i + 1 if i % 2 else i - 1) % lines) for i in range(lines)]

    pairs = [
        (2 * src + c, 2 * dst + c) for c, swaps in enumerate((left_pairs, right_pairs)) for src, dst in swaps
    ]

    def swap_near(top, low):
        return (lax.ppermute(top, ("k", "p"), left_pairs), lax.ppermute(low, ("k", "p"), right_pairs))

    kind = token_class.astype(BF16).reshape(2, mine, 1)
    tail = jnp.broadcast_to(jnp.concatenate([kind, kind], axis=1), (2, rows, BLOCK))
    pair = jnp.concatenate([tokens.reshape(2, mine, half), cotangent.reshape(2, mine, half)], axis=1)
    pair = jnp.concatenate([pair, tail], axis=2)
    pair = jnp.broadcast_to(pair[None], (zs, 2, rows, half + BLOCK)).reshape(zs * 2, rows, half + BLOCK)
    pair, mantissas, exponents = lax.optimization_barrier((pair, mantissas, exponents))
    near = lax.all_to_all(pair, ("z", "c"), 0, 0, tiled=True)

    raw_other, exponents_other = lax.ppermute(mantissas, "c", SWAP), lax.ppermute(exponents, "c", SWAP)

    def dequant(raw, powers, name):
        scale = jnp.exp2(powers.astype(F32)).astype(BF16).astype(F32)
        return call(dequant_kernel, name, jax.ShapeDtypeStruct(raw.shape, BF16), (scale, raw),
                    smem=(0,), flops=raw.size, moved=4 * raw.size)

    own = dequant(mantissas, exponents, "dequant_own")
    other = dequant(raw_other, exponents_other, "dequant_other")

    place = jnp.stack([core, lax.axis_index("z")])
    near, own, other, odd, place = lax.optimization_barrier((near, own, other, odd, place))
    masked = call(spread_kernel, "spread", jax.ShapeDtypeStruct((xs, zs, rows, 2 * half), BF16), (place, class_bands, near),
                  smem=(0, 1), moved=2 << 20)
    gathered = lax.all_to_all(masked, "x", 0, 0, tiled=True).reshape(bands, rows, 2 * half)

    work = count * mats * units * 2 * half

    def shape(*dims):
        return jax.ShapeDtypeStruct(dims, BF16)

    dy_own, dy_other, keep, send = call(
        project_kernel, "project", (shape(count, half),) * 2 + (shape(ks, 3 * chunk, units),) * 2,
        (odd, gathered, own, other), smem=(0,), flops=2 * work, moved=10 << 20)
    parts = (keep.astype(F32) + lax.ppermute(send, ("k", "p", "c"), pairs).astype(F32)).astype(BF16)
    parts = lax.all_to_all(parts, "k", 0, 0, tiled=True)
    acts = call(activate_kernel, "activate", shape(*parts.shape), (parts,), flops=parts.size, moved=4 * parts.size)
    acts = lax.all_to_all(acts, "k", 0, 0, tiled=True)
    top, low = swap_near(acts[: ks // 2], acts[ks // 2 :])
    terms, hidden = call(expand_kernel, "expand", (shape(bands, rows, 2 * half), shape(count, units)),
                         (odd, acts, top, low, own, other), smem=(0,), flops=2 * work, moved=10 << 20)

    terms = lax.all_to_all(terms.reshape(xs, zs, rows, 2 * half), "x", 0, 0, tiled=True)
    terms = call(gather_sum_kernel, "gather_sum", shape(zs * 2, rows, half), (core.reshape(1), terms),
                 smem=(0,), moved=1 << 20)
    terms, hidden, dy_other = lax.optimization_barrier((terms, hidden, dy_other))
    terms = lax.all_to_all(terms, ("z", "c"), 0, 0, tiled=True).reshape(zs, 2, rows, half)
    total = jnp.sum(terms.astype(F32), axis=0).astype(BF16)
    mixed = total[:, :mine].reshape(rows, half)
    input_grad = total[:, mine:].reshape(rows, half)

    norm_factor = 1.0 / jnp.sqrt(jnp.float32(2 * count))
    dy_got, got = lax.ppermute(dy_other, "c", SWAP), lax.ppermute(hidden, "c", SWAP)
    down = lax.dot_general(jnp.concatenate([hidden, got]), jnp.concatenate([dy_own, dy_got]), TN,
                           preferred_element_type=F32)
    down_grad = (down * norm_factor).astype(BF16)
    return mixed, input_grad, down_grad


def solution(mesh):
    dp, tensor = mesh.devices.shape
    split = Mesh(mesh.devices.reshape(dp // X_CHIPS, X_CHIPS, tensor // 4, 2, 2), ("z", "x", "k", "p", "c"))
    toks, cols = ("z", "x"), ("k", "p", "c")
    in_specs = (
        P(toks, cols),
        P(toks, cols),
        P(toks),
        P(),
        P(None, toks, cols),
        P(None, toks, cols),
    )
    out_specs = (P(toks, cols), P(toks, cols), P(toks, cols))
    return jax.shard_map(body, mesh=split, in_specs=in_specs, out_specs=out_specs, check_vma=False)
```
